32 devices in a mesh: seq: 8 (over z, core), mp: 4 (over y, x).
Axes of the slice: x: 2, y: 2, z: 4, core: 2. Of those that a mesh axis runs over, the one named last changes fastest.
Arguments:
- tokens_in: bfloat16 [16384, 2048], P('seq'), may hold values from -6 to 6
- norm_gain: float32 [2048], replicated, may hold values from 0.5 to 200
- q_weight: bfloat16 [2048, 2048], P('seq', 'mp'), may hold values from -0.125 to 0.125
- kv_weight: bfloat16 [4, 2048, 128], P(None, 'seq'), may hold values from -0.125 to 0.125
- out_weight: bfloat16 [2048, 2048], P('seq', 'mp'), may hold values from -0.25 to 0.25
- segment_ids: int32 [16384], P('seq'), may hold values from 0 to 15, never falling along the last dimension, each value on 1 to 4096 neighbouring positions
- page_table: int32 [128], P('seq'), may hold values from 0 to 127, as said below
Outputs:
- layer_out: bfloat16 [16384, 2048], P('seq', 'mp')
- kv_cache: bfloat16 [128, 512, 128], P('seq', 'mp')
The draws below stay inside these ranges and needn't reach their ends.
Inputs may be any that keep to these rules, and one draw needn't show every extreme that they name: `segment_ids`: segment numbers never fall along the stream; each of the 16 segments holds 1 to 4096 tokens and one holds exactly 4096. `page_table`: A permutation of the 128 cache slots; slot s belongs to index s // 16 of seq. The pages of index i of seq go to the indices i + o, counted round, for 8 distinct offsets o that are the same for every i, among them 1 and 8 / 2; exactly 2 pages to each owner.
All inputs are finite; a program needn't handle non-finite values.
Results may differ from the reference program's by a relative error of at most 0.018.
The reference program's roundings to bfloat16 on the way count: a program that leaves them out, or rounds other values in their place, can miss the bound.
Values may be sent and summed in bfloat16 or wider, within the bound.
A program may use at most 128 MiB of HBM per device.

```python
import math
import jax
import jax.numpy as jnp
import numpy as np
from jax import lax

D = 2048
H = 32
HD = 64
KVH = 4
W = 2048
PAGE = 128
TOK_DEV = 2048
TOKENS = 16384
SEGS = 16
MOST = 4096
PAGES_DEV = 16
NPAGES = 128
SPREAD = 8
CAP = 2
N_SEQ = 8
N_MP = 4


def draw_norm_gain(key, part):
    first_key = jax.random.fold_in(key, 0)
    gains = jnp.exp(jax.random.uniform(first_key, (D,), jnp.float32, math.log(0.5), math.log(2.0)))
    return gains


def draw_page_table(key, part):
    first_key, second_key = jax.random.split(key)
    order_all = jax.random.permutation(first_key, N_SEQ).astype(jnp.int32)
    where_one = jnp.argmax(order_all == 1)
    order_all = order_all.at[where_one].set(order_all[0])
    order_all = order_all.at[0].set(1)
    halfway = N_SEQ // 2
    if halfway != 1:
        where_half = jnp.argmax(order_all == halfway)
        order_all = order_all.at[where_half].set(order_all[1])
        order_all = order_all.at[1].set(halfway)
    offsets = order_all[:SPREAD]
    lane_keys = jax.random.split(second_key, N_SEQ)
    lanes = jax.vmap(lambda one_key: jax.random.permutation(one_key, PAGES_DEV))(lane_keys).astype(jnp.int32)
    sources = jnp.arange(N_SEQ, dtype=jnp.int32)[:, None]
    hops = lanes // CAP
    owners = (sources + offsets[hops]) % N_SEQ
    slots = owners * PAGES_DEV + hops * CAP + lanes % CAP
    return slots.reshape(-1).astype(jnp.int32)


def level_of(own_key, shape, shards, smallest, top_value):
    level, own = 1.0, jax.random.fold_in(own_key, 6)
    for position, parts in shards:
        steps = jnp.exp(jax.random.uniform(jax.random.fold_in(own, position), (parts,), jnp.float32, smallest / len(shards), top_value / len(shards)))
        level = level * jnp.repeat(steps, shape[position] // parts).reshape([-1 if axis == position else 1 for axis in range(len(shape))])
    return level


def profile(number_of, total, limit, lean):
    weights = [(1 << 20) // math.isqrt(rank ** lean) + 1 for rank in range(2, number_of + 1)]
    spare, counts = total - limit - (number_of - 1), [1] * (number_of - 1)
    while spare > 0:
        movable = [i for i in range(number_of - 1) if counts[i] < limit]
        whole, remaining = sum([weights[i] for i in movable]), spare
        for i in movable:
            more = min(limit - counts[i], max(1, remaining * weights[i] // whole), spare)
            counts[i] = counts[i] + more
            spare = spare - more
    return np.array([limit] + counts)


def uneven(stream_key, number_of, total, bound, slope):
    if number_of == 2:
        one = jax.random.randint(stream_key, (), max(1, total - bound), min(bound, total - 1) + 1)
        return jnp.stack([one, total - one])
    sizes = jnp.asarray(profile(number_of, total, bound, slope), jnp.int32)
    couples = (number_of - 1) // 2
    giver, sink = sizes[1:1 + 2 * couples:2], sizes[2:2 + 2 * couples:2]
    slack = jnp.minimum(giver - 1, bound - sink)
    shifted = jax.random.randint(jax.random.fold_in(stream_key, 1), (couples,), 0, 1 << 20) % (slack + 1)
    sizes = sizes.at[1:1 + 2 * couples:2].set(giver - shifted).at[2:2 + 2 * couples:2].set(sink + shifted)
    return sizes[jax.random.permutation(jax.random.fold_in(stream_key, 2), number_of)]


def normal_values(key, extent, deviation, limit, pieces=(), held_as=jnp.bfloat16):
    level = level_of(key, extent, pieces, -0.22, 0.18) if pieces else 1.0
    entries = jax.random.normal(key, extent, jnp.float32) * deviation * level
    return jnp.minimum(jnp.maximum(entries, -limit), limit).astype(held_as)


def setup_inputs(seed: int = 0) -> dict:
    streams_of = jax.random.split(jax.random.key(seed), 8)
    tokens_in = normal_values(streams_of[0], (TOKENS, D), 1.0, 6.0, ((0, 8),))
    norm_gain = draw_norm_gain(jax.random.fold_in(streams_of[7], 71), 0)
    q_weight = normal_values(streams_of[2], (D, H * HD), D ** -0.5, 0.125, ((0, 8), (1, 4)))
    kv_weight = normal_values(streams_of[3], (KVH, D, 2 * HD), D ** -0.5, 0.125, ((1, 8),))
    out_weight = normal_values(streams_of[4], (D, H * HD), (H * HD // 4) ** -0.5, 0.25, ((0, 8), (1, 4)))
    segment_ids = jnp.searchsorted(jnp.cumsum(uneven(streams_of[5], SEGS, TOKENS, MOST, 2)), jnp.arange(TOKENS), side="right").astype(jnp.int32)
    page_table = draw_page_table(jax.random.fold_in(streams_of[7], 71), 0)
    return {"tokens_in": tokens_in, "norm_gain": norm_gain, "q_weight": q_weight, "kv_weight": kv_weight, "out_weight": out_weight, "segment_ids": segment_ids, "page_table": page_table}


def rotate_half(values, cosine, sine_table):
    half = values.shape[-1] // 2
    first_half = values[..., :half]
    second = values[..., half:]
    return jnp.concatenate([first_half * cosine - second * sine_table, second * cosine + first_half * sine_table], axis=-1)

def angle_tables(positions):
    half = HD // 2
    freqs = jnp.exp(jnp.arange(half, dtype=jnp.float32) * (-2.0 * math.log(10000.0) / HD))
    angles = positions.astype(jnp.float32)[:, None] * freqs[None, :]
    return (jnp.cos(angles), jnp.sin(angles))

def reference(tokens_in, norm_gain, q_weight, kv_weight, out_weight, segment_ids, page_table):
    inputs = tokens_in.astype(jnp.float32)
    meansq = lax.optimization_barrier(jnp.mean(inputs * inputs, axis=-1, keepdims=True))
    normed = (inputs * lax.rsqrt(meansq + 1e-05) * norm_gain).astype(jnp.bfloat16)
    indices = jnp.arange(TOKENS, dtype=jnp.int32)
    boundary = jnp.concatenate([jnp.ones((1,), bool), segment_ids[1:] != segment_ids[:-1]])
    starts = lax.cummax(jnp.where(boundary, indices, jnp.int32(0)), axis=0)
    positions = indices - starts
    cosine, sine_table = angle_tables(positions)
    queries = jnp.dot(normed, q_weight, preferred_element_type=jnp.float32).reshape(TOKENS, H, HD)
    queries = rotate_half(queries, cosine[:, None, :], sine_table[:, None, :]).astype(jnp.bfloat16)
    kv_flat = kv_weight.transpose(1, 0, 2).reshape(D, KVH * 2 * HD)
    projected = jnp.dot(normed, kv_flat, preferred_element_type=jnp.float32).reshape(TOKENS, KVH, 2 * HD)
    key_rows = rotate_half(projected[..., :HD], cosine[:, None, :], sine_table[:, None, :]).astype(jnp.bfloat16)
    value_rows = projected[..., HD:].astype(jnp.bfloat16)
    group = H // KVH
    block_rows = min(512, TOK_DEV)
    blocks = TOKENS // block_rows
    key_padded = jnp.concatenate([jnp.zeros((W, KVH, HD), jnp.bfloat16), key_rows], axis=0)
    value_padded = jnp.concatenate([jnp.zeros((W, KVH, HD), jnp.bfloat16), value_rows], axis=0)
    scale = 1.0 / math.sqrt(HD)

    def one_block(block):
        row_first = block * block_rows
        query_block = lax.dynamic_slice_in_dim(queries, row_first, block_rows, 0).astype(jnp.float32)
        query_block = query_block.reshape(block_rows, KVH, group, HD)
        key_block = lax.dynamic_slice_in_dim(key_padded, row_first, W + block_rows, 0).astype(jnp.float32)
        value_block = lax.dynamic_slice_in_dim(value_padded, row_first, W + block_rows, 0).astype(jnp.float32)
        key_index = row_first - W + jnp.arange(W + block_rows, dtype=jnp.int32)
        query_index = row_first + jnp.arange(block_rows, dtype=jnp.int32)
        query_start = lax.dynamic_slice_in_dim(starts, row_first, block_rows, 0)
        scores = jnp.einsum('qjgd,kjd->jgqk', query_block, key_block) * scale
        keep = (key_index[None, :] >= query_start[:, None]) & (key_index[None, :] <= query_index[:, None])
        keep = keep & (query_index[:, None] - key_index[None, :] < W)
        masked = jnp.where(keep[None, None], scores, -1e+30)
        highest = lax.optimization_barrier(jnp.max(masked, axis=-1, keepdims=True))
        weights = jnp.where(keep[None, None], jnp.exp(masked - highest), 0.0)
        probs = (weights / lax.optimization_barrier(jnp.sum(weights, axis=-1, keepdims=True))).astype(jnp.bfloat16)
        mixed = jnp.einsum('jgqk,kjd->qjgd', probs.astype(jnp.float32), value_block)
        return mixed.reshape(block_rows, H * HD).astype(jnp.bfloat16)
    attended = lax.map(one_block, jnp.arange(blocks, dtype=jnp.int32)).reshape(TOKENS, H * HD)
    columns = H * HD // N_MP
    total = jnp.zeros((TOKENS, D), jnp.float32)
    for group_index in range(N_MP):
        lower = group_index * columns
        partial_term = jnp.dot(attended[:, lower:lower + columns], out_weight[:, lower:lower + columns].T, preferred_element_type=jnp.float32)
        rounded = lax.optimization_barrier(partial_term.astype(jnp.bfloat16))
        total = total + rounded.astype(jnp.float32)
    layer_out = total.astype(jnp.bfloat16)
    combined = jnp.concatenate([key_rows, value_rows], axis=-1).reshape(TOKENS, KVH * 2 * HD)
    page_blocks = combined.reshape(NPAGES, PAGE, KVH * 2 * HD).transpose(0, 2, 1)
    kv_cache = jnp.zeros_like(page_blocks).at[page_table].set(page_blocks)
    return (layer_out, kv_cache)
```

```python
import functools
import math

import jax
import jax.numpy as jnp
from jax import lax
from jax.experimental import pallas as pl
from jax.experimental.pallas import tpu as pltpu
from jax.sharding import PartitionSpec as P

W = 2048
PAGE = 128
BINS = 128
BQ = 256
BK = 768
CHUNKS = (512, 512, 512, 512)
LOG2E = 1.4426950408889634


def attend_kernel(heads, head_size, first, tok_rows, lows, low_ref, q_ref, k_ref, v_ref, o_ref,
                  q_scr, bias_scr, m_scr, acc_scr):
    block = pl.program_id(0)
    q0 = tok_rows + first + block * BQ
    end = q0 + BQ
    scale = LOG2E / math.sqrt(head_size)
    for h in range(heads):
        scaled = q_ref[h * head_size:(h + 1) * head_size, :].astype(jnp.float32) * scale
        high = scaled.astype(jnp.bfloat16)
        q_scr[h, :head_size, :] = high
        q_scr[h, head_size:, :] = (scaled - high.astype(jnp.float32)).astype(jnp.bfloat16)
    m_scr[...] = jnp.full_like(m_scr, -1e30)
    acc_scr[...] = jnp.zeros_like(acc_scr)
    low = low_ref[...]
    query = q0 + lax.broadcasted_iota(jnp.int32, (1, BQ), 1)
    steps = (end - lows[first // BQ + block] + BK - 1) // BK

    def step(j, carry):
        k0 = pl.multiple_of(end - (j + 1) * BK, 256)
        keys = k_ref[pl.ds(k0, BK), :]
        vals = v_ref[:, pl.ds(k0, BK)]
        key = k0 + lax.broadcasted_iota(jnp.int32, (BK, 1), 0)
        bias_scr[...] = jnp.where((key >= low) & (key <= query), 0.0, -1e30)

        def score(h):
            return jnp.dot(keys, q_scr[h], preferred_element_type=jnp.float32)

        s = score(0)
        for h in range(heads):
            following = score(h + 1) if h + 1 < heads else None
            s = s + bias_scr[...]
            old = m_scr[h]
            new = jnp.maximum(old, jnp.max(s, axis=0, keepdims=True))
            p = jnp.exp2(s - new).astype(jnp.bfloat16)
            mixed = jnp.dot(vals, p, preferred_element_type=jnp.float32)
            acc_scr[h] = acc_scr[h] * jnp.exp2(old - new) + mixed
            m_scr[h] = new
            s = following
        return carry

    lax.fori_loop(0, steps, step, 0)
    for h in range(heads):
        total = acc_scr[h, head_size:head_size + 1, :]
        o_ref[h * head_size:(h + 1) * head_size, :] = (
            acc_scr[h, :head_size, :] / total
        ).astype(jnp.bfloat16)


def attend(lows, low, q_t, keys, vals, first, count, heads, head_size):
    tok_rows = q_t.shape[1]
    off = first // BQ
    whole = lambda a: pl.BlockSpec(a.shape, lambda i, s: (0, 0))
    return pl.pallas_call(
        functools.partial(attend_kernel, heads, head_size, first, tok_rows),
        out_shape=jax.ShapeDtypeStruct((heads * head_size, count), jnp.bfloat16),
        grid_spec=pltpu.PrefetchScalarGridSpec(
            num_scalar_prefetch=1,
            grid=(count // BQ,),
            in_specs=[
                pl.BlockSpec((1, BQ), lambda i, s: (0, off + i)),
                pl.BlockSpec((heads * head_size, BQ), lambda i, s: (0, off + i)),
                whole(keys),
                whole(vals),
            ],
            out_specs=pl.BlockSpec((heads * head_size, BQ), lambda i, s: (0, i)),
            scratch_shapes=[
                pltpu.VMEM((heads, 2 * head_size, BQ), jnp.bfloat16),
                pltpu.VMEM((BK, BQ), jnp.float32),
                pltpu.VMEM((heads, 1, BQ), jnp.float32),
                pltpu.VMEM((heads, vals.shape[0], BQ), jnp.float32),
            ],
        ),
        compiler_params=pltpu.CompilerParams(vmem_limit_bytes=48 << 20),
        cost_estimate=pl.CostEstimate(
            flops=count * 2048 * heads * 256 * 2 * 2,
            bytes_accessed=6 << 20,
            transcendentals=count * 2304 * heads,
        ),
    )(lows, low, q_t, keys, vals)


def pick_kernel(pages, order, src, dst):
    for lane in range(pages):
        col = pl.multiple_of(order[lane] * PAGE, PAGE)
        dst[lane] = src[:, pl.ds(col, PAGE)]


def place_kernel(pages, order, src, dst):
    for slot in range(pages):
        dst[slot] = src[order[slot]]


def reorder(kernel, order, src, pages, rows):
    return pl.pallas_call(
        functools.partial(kernel, pages),
        out_shape=jax.ShapeDtypeStruct((pages, rows, PAGE), src.dtype),
        in_specs=[
            pl.BlockSpec(memory_space=pltpu.SMEM),
            pl.BlockSpec(memory_space=pltpu.VMEM),
        ],
        out_specs=pl.BlockSpec(memory_space=pltpu.VMEM),
        cost_estimate=pl.CostEstimate(flops=0, bytes_accessed=1 << 20, transcendentals=0),
    )(order, src)


def rotate(v, cosine, sine):
    half = v.shape[-2] // 2
    a, b = v[..., :half, :], v[..., half:, :]
    return jnp.concatenate([a * cosine - b * sine, b * cosine + a * sine], axis=-2)


def body(tokens_in, norm_gain, q_weight, kv_weight, out_weight, segment_ids, page_table):
    seq_count = lax.axis_size("seq")
    mp_count = lax.axis_size("mp")
    seq_index = lax.axis_index("seq")
    mp_index = lax.axis_index("mp")
    tok_rows = tokens_in.shape[0]
    kv_heads = kv_weight.shape[0]
    head_size = kv_weight.shape[2] // 2
    assert tok_rows == W
    ratio = mp_count // kv_heads
    share_width = 2 * head_size // ratio
    pages_dev = tok_rows // PAGE
    capacity = pages_dev // seq_count

    with jax.named_scope("gathers"):
        bins = jnp.arange(BINS, dtype=jnp.int32)
        below = jnp.sum((segment_ids[None, :] < bins[:, None]).astype(jnp.int32), axis=1)
        padded = jnp.pad(page_table, (0, BINS - pages_dev))
        info = lax.all_gather(jnp.stack([below, padded]), "seq")
        kv_own = lax.dynamic_index_in_dim(kv_weight, mp_index // ratio, 0, keepdims=False)
        w_keyval = lax.all_gather(kv_own, "seq", axis=0, tiled=True)
        w_query = lax.all_gather(q_weight, "seq", axis=0, tiled=True)
        late, w_query = lax.optimization_barrier((out_weight, w_query))
        w_output = lax.all_gather(late, "seq", axis=0, tiled=True)

    with jax.named_scope("norm"):
        inputs = tokens_in.astype(jnp.float32)
        meansq = jnp.mean(inputs * inputs, axis=-1, keepdims=True)
        normed = (inputs * lax.rsqrt(meansq + 1e-05) * norm_gain).astype(jnp.bfloat16)

    with jax.named_scope("positions"):
        starts = jnp.sum(info[:, 0, :], axis=0)
        one_hot = segment_ids[None, :] == bins[:, None]
        query_start = jnp.sum(jnp.where(one_hot, starts[:, None], 0), axis=0)
        token_first = seq_index * tok_rows
        local = jnp.arange(tok_rows, dtype=jnp.int32)
        positions = token_first + local - query_start
        half = head_size // 2
        freqs = jnp.exp(
            jnp.arange(half, dtype=jnp.float32) * (-2.0 * math.log(10000.0) / head_size)
        )
        angles = positions.astype(jnp.float32)[None, :] * freqs[:, None]
        cosine, sine = jnp.cos(angles), jnp.sin(angles)
        low = jnp.maximum(query_start - token_first + tok_rows, local + tok_rows - W + 1)
        lows = low[::BQ]

    with jax.named_scope("keyval"):
        kv_t = lax.dot_general(
            w_keyval, normed, (((0,), (1,)), ((), ())), preferred_element_type=jnp.float32
        )
        kv_t = jnp.concatenate(
            [rotate(kv_t[:head_size], cosine, sine), kv_t[head_size:]], axis=0
        ).astype(jnp.bfloat16)
        behind = lax.ppermute(kv_t, "seq", [(i, i + 1) for i in range(seq_count - 1)])

    with jax.named_scope("queries"):
        heads = w_query.shape[1] // head_size
        q_t = lax.dot_general(
            w_query, normed, (((0,), (1,)), ((), ())), preferred_element_type=jnp.float32
        ).reshape(heads, head_size, tok_rows)
        q_t = rotate(q_t, cosine, sine).astype(jnp.bfloat16).reshape(heads * head_size, tok_rows)

    with jax.named_scope("pages_out"):
        owners = page_table // pages_dev
        order = jnp.arange(pages_dev, dtype=jnp.int32)
        rank = jnp.sum(
            ((owners[:, None] == owners[None, :]) & (order[None, :] < order[:, None])).astype(
                jnp.int32
            ),
            axis=1,
        )
        lane = lax.rem(owners - seq_index + seq_count, seq_count) * capacity + rank
        page_of_lane = jnp.sum(
            jnp.where(lane[None, :] == order[:, None], order[None, :], 0), axis=1
        )
        share = lax.dynamic_slice_in_dim(
            kv_t, lax.rem(mp_index, ratio) * share_width, share_width, 0
        )
        outgoing = reorder(pick_kernel, page_of_lane, share, pages_dev, share_width)
        arrived = [outgoing[:capacity]]
        for d in range(1, seq_count):
            arrived.append(
                lax.ppermute(
                    outgoing[d * capacity:(d + 1) * capacity],
                    "seq",
                    [(i, (i + d) % seq_count) for i in range(seq_count)],
                )
            )

    with jax.named_scope("attention"):
        both = jnp.concatenate([behind, kv_t], axis=1)
        key_rows = both[:head_size].T
        keys = jnp.concatenate([key_rows, key_rows], axis=1)
        vals = jnp.concatenate(
            [both[head_size:], jnp.ones((16, 2 * tok_rows), jnp.bfloat16)], axis=0
        )
        low_row = low[None, :]
        outs, first = [], 0
        for count in CHUNKS:
            att = attend(lows, low_row, q_t, keys, vals, first, count, heads, head_size)
            part = lax.dot_general(
                att, w_output, (((0,), (1,)), ((), ())), preferred_element_type=jnp.float32
            ).astype(jnp.bfloat16)
            outs.append(lax.psum_scatter(part, "mp", scatter_dimension=1, tiled=True))
            first += count
        layer_out = jnp.concatenate(outs, axis=0)

    with jax.named_scope("pages_in"):
        tables = info[:, 1, :pages_dev]
        mine = (tables // pages_dev) == seq_index
        before = jnp.sum(
            jnp.where(order[None, None, :] < order[None, :, None], mine[:, None, :], False).astype(
                jnp.int32
            ),
            axis=2,
        )
        source = jnp.arange(seq_count, dtype=jnp.int32)[:, None]
        shift = lax.rem(seq_index - source + seq_count, seq_count)
        lane_in = jnp.where(mine, shift * capacity + before, 0)
        slot_in = jnp.where(mine, tables % pages_dev, -1)
        lane_of_slot = jnp.sum(
            jnp.where(slot_in[None] == order[:, None, None], lane_in[None], 0), axis=(1, 2)
        )
        kv_cache = reorder(
            place_kernel, lane_of_slot, jnp.concatenate(arrived, axis=0), pages_dev, share_width
        )
    return (layer_out, kv_cache)


def solution(mesh):
    placed = (
        P("seq", None),
        P(),
        P("seq", "mp"),
        P(None, "seq", None),
        P("seq", "mp"),
        P("seq"),
        P("seq"),
    )
    return jax.shard_map(
        body,
        mesh=mesh,
        in_specs=placed,
        out_specs=(P("seq", "mp"), P("seq", "mp", None)),
        check_vma=False,
    )
```

```python
import functools
import math

import jax
import jax.numpy as jnp
from jax import lax
from jax.experimental import pallas as pl
from jax.experimental.pallas import tpu as pltpu
from jax.sharding import PartitionSpec as P

W = 2048
PAGE = 128
BINS = 128
BQ = 256
BK = 768
CHUNKS = (512, 512, 512, 256, 256)
INFO_ROWS = 16
LOG2E = 1.4426950408889634


def attend_kernel(heads, head_size, first, tok_rows, lows, low_ref, q_ref, k_ref, v_ref, o_ref,
                  q_scr, bias_scr, m_scr, acc_scr):
    block = pl.program_id(0)
    q0 = tok_rows + first + block * BQ
    end = q0 + BQ
    scale = LOG2E / math.sqrt(head_size)
    for h in range(heads):
        scaled = q_ref[h * head_size:(h + 1) * head_size, :].astype(jnp.float32) * scale
        high = scaled.astype(jnp.bfloat16)
        q_scr[h, :head_size, :] = high
        q_scr[h, head_size:, :] = (scaled - high.astype(jnp.float32)).astype(jnp.bfloat16)
    m_scr[...] = jnp.full_like(m_scr, -1e30)
    acc_scr[...] = jnp.zeros_like(acc_scr)
    low = low_ref[...]
    query = q0 + lax.broadcasted_iota(jnp.int32, (1, BQ), 1)
    steps = (end - lows[2 * (first // BQ + block)] + BK - 1) // BK

    def visit(k0, masked):
        keys = k_ref[pl.ds(k0, BK), :]
        vals = v_ref[:, pl.ds(k0, BK)]
        if masked:
            key = k0 + lax.broadcasted_iota(jnp.int32, (BK, 1), 0)
            bias_scr[...] = jnp.where((key >= low) & (key <= query), 0.0, -1e30)

        def score(h):
            return jnp.dot(keys, q_scr[h], preferred_element_type=jnp.float32)

        s = score(0)
        for h in range(heads):
            following = score(h + 1) if h + 1 < heads else None
            if masked:
                s = s + bias_scr[...]
            old = m_scr[h]
            new = jnp.maximum(old, jnp.max(s, axis=0, keepdims=True))
            p = jnp.exp2((s - new).astype(jnp.bfloat16))
            mixed = jnp.dot(vals, p, preferred_element_type=jnp.float32)
            acc_scr[h] = acc_scr[h] * jnp.exp2(old - new) + mixed
            m_scr[h] = new
            s = following

    def step(j, carry):
        k0 = pl.multiple_of(end - (j + 1) * BK, 256)
        clean = (k0 + BK - 1 <= q0) & (k0 >= lows[2 * (first // BQ + block) + 1])

        @pl.when(clean)
        def _():
            visit(k0, False)

        @pl.when(jnp.logical_not(clean))
        def _():
            visit(k0, True)

        return carry

    lax.fori_loop(0, steps, step, 0)
    for h in range(heads):
        total = acc_scr[h, head_size:head_size + 1, :]
        o_ref[h * head_size:(h + 1) * head_size, :] = (
            acc_scr[h, :head_size, :] / total
        ).astype(jnp.bfloat16)


def attend(lows, low, q_t, keys, vals, first, count, heads, head_size):
    tok_rows = q_t.shape[1]
    off = first // BQ
    whole = lambda a: pl.BlockSpec(a.shape, lambda i, s: (0, 0))
    return pl.pallas_call(
        functools.partial(attend_kernel, heads, head_size, first, tok_rows),
        out_shape=jax.ShapeDtypeStruct((heads * head_size, count), jnp.bfloat16),
        grid_spec=pltpu.PrefetchScalarGridSpec(
            num_scalar_prefetch=1,
            grid=(count // BQ,),
            in_specs=[
                pl.BlockSpec((1, BQ), lambda i, s: (0, off + i)),
                pl.BlockSpec((heads * head_size, BQ), lambda i, s: (0, off + i)),
                whole(keys),
                whole(vals),
            ],
            out_specs=pl.BlockSpec((heads * head_size, BQ), lambda i, s: (0, i)),
            scratch_shapes=[
                pltpu.VMEM((heads, 2 * head_size, BQ), jnp.bfloat16),
                pltpu.VMEM((BK, BQ), jnp.float32),
                pltpu.VMEM((heads, 1, BQ), jnp.float32),
                pltpu.VMEM((heads, vals.shape[0], BQ), jnp.float32),
            ],
        ),
        compiler_params=pltpu.CompilerParams(vmem_limit_bytes=48 << 20),
        cost_estimate=pl.CostEstimate(
            flops=count * 2048 * heads * 256 * 2 * 2,
            bytes_accessed=6 << 20,
            transcendentals=count * 2304 * heads,
        ),
    )(lows, low, q_t, keys, vals)


def pick_kernel(pages, order, src, dst):
    for lane in range(pages):
        col = pl.multiple_of(order[lane] * PAGE, PAGE)
        dst[lane] = src[:, pl.ds(col, PAGE)]


def place_kernel(pages, order, src, dst):
    for slot in range(pages):
        dst[slot] = src[order[slot]]


def reorder(kernel, order, src, pages, rows):
    return pl.pallas_call(
        functools.partial(kernel, pages),
        out_shape=jax.ShapeDtypeStruct((pages, rows, PAGE), src.dtype),
        in_specs=[
            pl.BlockSpec(memory_space=pltpu.SMEM),
            pl.BlockSpec(memory_space=pltpu.VMEM),
        ],
        out_specs=pl.BlockSpec(memory_space=pltpu.VMEM),
        cost_estimate=pl.CostEstimate(flops=0, bytes_accessed=1 << 20, transcendentals=0),
    )(order, src)


def rotate(v, cosine, sine):
    half = v.shape[-2] // 2
    a, b = v[..., :half, :], v[..., half:, :]
    return jnp.concatenate([a * cosine - b * sine, b * cosine + a * sine], axis=-2)


def joined(terms):
    total = terms[0].astype(jnp.float32)
    for part in terms[1:]:
        total = total + part.astype(jnp.float32)
    return total.astype(jnp.bfloat16)


def body(tokens_in, norm_gain, q_weight, kv_weight, out_weight, segment_ids, page_table):
    seq_count = lax.axis_size("seq")
    mp_count = lax.axis_size("mp")
    seq_index = lax.axis_index("seq")
    mp_index = lax.axis_index("mp")
    tok_rows = tokens_in.shape[0]
    kv_heads = kv_weight.shape[0]
    head_size = kv_weight.shape[2] // 2
    assert tok_rows == W
    ratio = mp_count // kv_heads
    share_width = 2 * head_size // ratio
    pages_dev = tok_rows // PAGE
    capacity = pages_dev // seq_count

    with jax.named_scope("gathers"):
        bins = jnp.arange(BINS, dtype=jnp.int32)
        below = jnp.sum((segment_ids[None, :] < bins[:, None]).astype(jnp.int32), axis=1)
        info = jnp.concatenate(
            [
                (below // 64)[None],
                (below % 64)[None],
                jnp.pad(page_table, (0, BINS - pages_dev))[None],
                jnp.zeros((INFO_ROWS - 3, BINS), jnp.int32),
            ]
        ).astype(jnp.bfloat16)
        kv_own = lax.dynamic_index_in_dim(kv_weight, mp_index // ratio, 0, keepdims=False)
        first_pack = lax.all_gather(jnp.concatenate([kv_own, info]), "seq")
        rows = kv_own.shape[0]
        w_keyval = first_pack[:, :rows].reshape(seq_count * rows, 2 * head_size)
        info = first_pack[:, rows:].astype(jnp.float32).astype(jnp.int32)
        w_query = lax.all_gather(q_weight, "seq", axis=0, tiled=True)
        late, w_query = lax.optimization_barrier((out_weight, w_query))
        w_output = lax.all_gather(late, "seq", axis=0, tiled=True)

    with jax.named_scope("norm"):
        inputs = tokens_in.astype(jnp.float32)
        meansq = jnp.mean(inputs * inputs, axis=-1, keepdims=True)
        normed = (inputs * lax.rsqrt(meansq + 1e-05) * norm_gain).astype(jnp.bfloat16)

    with jax.named_scope("positions"):
        starts = jnp.sum(info[:, 0, :] * 64 + info[:, 1, :], axis=0)
        one_hot = segment_ids[None, :] == bins[:, None]
        query_start = jnp.sum(jnp.where(one_hot, starts[:, None], 0), axis=0)
        token_first = seq_index * tok_rows
        local = jnp.arange(tok_rows, dtype=jnp.int32)
        positions = token_first + local - query_start
        half = head_size // 2
        freqs = jnp.exp(
            jnp.arange(half, dtype=jnp.float32) * (-2.0 * math.log(10000.0) / head_size)
        )
        angles = positions.astype(jnp.float32)[None, :] * freqs[:, None]
        cosine, sine = jnp.cos(angles), jnp.sin(angles)
        low = jnp.maximum(query_start - token_first + tok_rows, local + tok_rows - W + 1)
        lows = jnp.stack([low[::BQ], low[BQ - 1::BQ]], axis=1).reshape(-1)

    with jax.named_scope("keyval"):
        kv_t = lax.dot_general(
            w_keyval, normed, (((0,), (1,)), ((), ())), preferred_element_type=jnp.float32
        )
        kv_t = jnp.concatenate(
            [rotate(kv_t[:head_size], cosine, sine), kv_t[head_size:]], axis=0
        ).astype(jnp.bfloat16)
        behind = lax.ppermute(kv_t, "seq", [(i, i + 1) for i in range(seq_count - 1)])

    with jax.named_scope("queries"):
        heads = w_query.shape[1] // head_size
        q_t = lax.dot_general(
            w_query, normed, (((0,), (1,)), ((), ())), preferred_element_type=jnp.float32
        ).reshape(heads, head_size, tok_rows)
        q_t = rotate(q_t, cosine, sine).astype(jnp.bfloat16).reshape(heads * head_size, tok_rows)

    with jax.named_scope("pages_out"):
        owners = page_table // pages_dev
        order = jnp.arange(pages_dev, dtype=jnp.int32)
        rank = jnp.sum(
            ((owners[:, None] == owners[None, :]) & (order[None, :] < order[:, None])).astype(
                jnp.int32
            ),
            axis=1,
        )
        lane = owners * capacity + rank
        page_of_lane = jnp.sum(
            jnp.where(lane[None, :] == order[:, None], order[None, :], 0), axis=1
        )
        share = lax.dynamic_slice_in_dim(
            kv_t, lax.rem(mp_index, ratio) * share_width, share_width, 0
        )
        outgoing = reorder(pick_kernel, page_of_lane, share, pages_dev, share_width)
        arrived = lax.all_to_all(outgoing, "seq", split_axis=0, concat_axis=0, tiled=True)

    with jax.named_scope("attention"):
        both = jnp.concatenate([behind, kv_t], axis=1)
        key_rows = both[:head_size].T
        keys = jnp.concatenate([key_rows, key_rows], axis=1)
        vals = jnp.concatenate(
            [both[head_size:], jnp.ones((16, 2 * tok_rows), jnp.bfloat16)], axis=0
        )
        low_row = low[None, :]
        width = w_output.shape[0] // mp_count
        w_parts = [
            lax.dynamic_slice_in_dim(w_output, (mp_index ^ d) * width, width, 0)
            for d in range(mp_count)
        ]
        outs, first, flying = [], 0, None
        for count in CHUNKS:
            att = attend(lows, low_row, q_t, keys, vals, first, count, heads, head_size)
            parts = [
                lax.dot_general(
                    att, w_parts[d], (((0,), (1,)), ((), ())), preferred_element_type=jnp.float32
                ).astype(jnp.bfloat16)
                for d in range(mp_count)
            ]
            low_row, parts = lax.optimization_barrier((low_row, parts))
            if first == 0:
                low_row, arrived = lax.optimization_barrier((low_row, arrived))
            if flying is not None:
                low_row, flying = lax.optimization_barrier((low_row, flying))
                outs.append(joined(flying))
            flying = [parts[0]] + [
                lax.ppermute(parts[d], "mp", [(i, i ^ d) for i in range(mp_count)])
                for d in range(1, mp_count)
            ]
            first += count
        outs.append(joined(flying))
        layer_out = jnp.concatenate(outs, axis=0)

    with jax.named_scope("pages_in"):
        tables = info[:, 2, :pages_dev]
        mine = (tables // pages_dev) == seq_index
        before = jnp.sum(
            jnp.where(order[None, None, :] < order[None, :, None], mine[:, None, :], False).astype(
                jnp.int32
            ),
            axis=2,
        )
        source = jnp.arange(seq_count, dtype=jnp.int32)[:, None]
        lane_in = jnp.where(mine, source * capacity + before, 0)
        slot_in = jnp.where(mine, tables % pages_dev, -1)
        lane_of_slot = jnp.sum(
            jnp.where(slot_in[None] == order[:, None, None], lane_in[None], 0), axis=(1, 2)
        )
        kv_cache = reorder(
            place_kernel, lane_of_slot, arrived, pages_dev, share_width
        )
    return (layer_out, kv_cache)


def solution(mesh):
    placed = (
        P("seq", None),
        P(),
        P("seq", "mp"),
        P(None, "seq", None),
        P("seq", "mp"),
        P("seq"),
        P("seq"),
    )
    return jax.shard_map(
        body,
        mesh=mesh,
        in_specs=placed,
        out_specs=(P("seq", "mp"), P("seq", "mp", None)),
        check_vma=False,
    )
```
